32 devices in a mesh: section: 2 (over core), row: 16 (over z, y, x).
Axes of the slice: x: 2, y: 2, z: 4, core: 2. Of those that a mesh axis runs over, the one named last changes fastest.
Arguments:
- node_features: float32 [3, 4096, 384], P(None, 'row'), may hold values from -6 to 6
- cotangent: float32 [3, 4096, 384], P(None, 'row'), may hold values from -6 to 6
- lengths: int32 [3], replicated, may hold values from 1024 to 4096, as said below
- neighbours: int32 [3, 27, 4096], P(None, None, 'row'), may hold values from 0 to 4095, as said below
- conv_weight: bfloat16 [2, 27, 384], P('section'), may hold values from -1.25 to 1.25
- norm_gains: bfloat16 [2, 3, 384], P('section'), may hold values from 0.5 to 1.5
- biases: bfloat16 [2, 5, 384], P('section'), may hold values from -2 to 2
- qkv_weight: bfloat16 [2, 384, 1152], P('section'), may hold values from -0.3125 to 0.3125
- out_weight: bfloat16 [2, 384, 384], P('section'), may hold values from -1.25 to 1.25
- up_weight: bfloat16 [2, 384, 1536], P('section'), may hold values from -0.3125 to 0.3125
- up_bias: bfloat16 [2, 1536], P('section'), may hold values from -2 to 2
- down_weight: bfloat16 [2, 1536, 384], P('section'), may hold values from -0.15625 to 0.15625
Outputs:
- block_out: float32 [2, 3, 4096, 384], P('section', None, 'row')
- input_grad: float32 [2, 3, 4096, 384], P('section', None, 'row')
- conv_grad: float32 [2, 27, 384], P('section')
- gains_grad: float32 [2, 3, 384], P('section')
- biases_grad: float32 [2, 5, 384], P('section')
- qkv_grad: float32 [2, 384, 1152], P('section')
- out_grad: float32 [2, 384, 384], P('section')
- up_grad: float32 [2, 384, 1536], P('section')
- up_bias_grad: float32 [2, 1536], P('section')
- down_grad: float32 [2, 1536, 384], P('section')
The draws below stay inside these ranges and needn't reach their ends.
Inputs may be any that keep to these rules, and one draw needn't show every extreme that they name: micro-batch m's valid nodes are its first lengths[m] rows; in every draw some micro-batch has all 4096 valid. `neighbours`: entry [m, k, i] is a node of micro-batch m at most 64 rows from node i; slot 13 is node i itself.
All inputs are finite; a program needn't handle non-finite values.
Results may differ from the reference program's by a relative error of at most 0.033.
Values may be sent and summed in bfloat16 or wider, within the bound.
No kernel may reach another device: no remote copies, remote signals or barrier semaphores. Data moves between devices by JAX's collectives and lax.ppermute only.
A program may use at most 256 MiB of HBM per device.

```python
import math
import jax
import jax.numpy as jnp
from jax import lax

C = 384
HEADS = 24
FF = 1536
HEAD = 16
WIN = 32
WINDOW_DILATION = 4
HALO = 64
MB = 3
NODES = 4096


def draw_lengths(key, part):
    key = jax.random.fold_in(key, 11)
    key_values, key_full = jax.random.split(key)
    drawn = jax.random.randint(key_values, (MB,), NODES // 4, NODES + 1)
    full_index = jax.random.randint(key_full, (), 0, MB)
    return jnp.where(jnp.arange(MB) == full_index, NODES, drawn).astype(jnp.int32)


def draw_neighbours(key, part):
    key = jax.random.fold_in(key, 7)
    offsets = jax.random.randint(key, (MB, 27, NODES), -HALO, HALO + 1)
    centre = (jnp.arange(27) == 13)[None, :, None]
    offsets = jnp.where(centre, 0, offsets)
    targets = jnp.arange(NODES)[None, None, :] + offsets
    return jnp.clip(targets, 0, NODES - 1).astype(jnp.int32)


def block_scale(own_key, dims, shards, low, top_value):
    level, own = 1.0, jax.random.fold_in(own_key, 6)
    for position, blocks in shards:
        draws = jnp.exp(jax.random.uniform(jax.random.fold_in(own, position), (blocks,), jnp.float32, low / len(shards), top_value / len(shards)))
        level = level * jnp.repeat(draws, dims[position] // blocks).reshape([-1 if axis == position else 1 for axis in range(len(dims))])
    return level


def normal_values(rng, dims, spread, reach, cuts=(), held_as=jnp.bfloat16):
    values = jax.random.normal(rng, dims, jnp.float32) * spread
    if len(cuts) > 0:
        values = block_scale(rng, dims, cuts, -0.22, 0.18) * values
    return jnp.clip(values, min=-reach, max=reach).astype(held_as)


def setup_inputs(seed: int = 0) -> dict:
    splits = jax.random.split(jax.random.key(seed), 13)
    return {
        "node_features": normal_values(splits[0], (MB, NODES, C), 1.0, 6.0, ((1, 16),), jnp.float32),
        "cotangent": normal_values(splits[1], (MB, NODES, C), 1.0, 6.0, ((1, 16),), jnp.float32),
        "lengths": draw_lengths(jax.random.fold_in(splits[12], 71), 0),
        "neighbours": draw_neighbours(jax.random.fold_in(splits[12], 71), 0),
        "conv_weight": normal_values(splits[4], (2, 27, C), 27 ** -0.5, 1.25, ((0, 2),)),
        "norm_gains": jnp.clip(1.0 + 0.1 * jax.random.normal(splits[5], (2, 3, C), jnp.float32), 0.5, 1.5).astype(jnp.bfloat16),
        "biases": normal_values(splits[6], (2, 5, C), 0.3, 2.0, ((0, 2),)),
        "qkv_weight": normal_values(splits[7], (2, C, 3 * C), C ** -0.5, 0.3125, ((0, 2),)),
        "out_weight": normal_values(splits[8], (2, C, C), (C // 16) ** -0.5, 1.25, ((0, 2),)),
        "up_weight": normal_values(splits[9], (2, C, FF), C ** -0.5, 0.3125, ((0, 2),)),
        "up_bias": normal_values(splits[10], (2, FF), 0.3, 2.0, ((0, 2),)),
        "down_weight": normal_values(splits[11], (2, FF, C), FF ** -0.5, 0.15625, ((0, 2),)),
    }


@jax.custom_vjp
def low(v):
    return lax.optimization_barrier(v.astype(jnp.bfloat16)).astype(jnp.float32)

@jax.custom_vjp
def low_back(v):
    return v

def low_keep(v):
    return (low(v), None)

def low_pass(kept, grad):
    return (grad,)

def back_keep(v):
    return (v, None)

def back_low(kept, grad):
    return (low(grad),)
low.defvjp(low_keep, low_pass)
low_back.defvjp(back_keep, back_low)
eps_value = 1e-05
mask_gap = 10000.0
highest = lax.Precision.HIGHEST

def round_both(value_rows):
    return low_back(low(value_rows))

def layer_norm(value_rows, gain_vec, offset):
    average = lax.optimization_barrier(jnp.mean(value_rows, -1, keepdims=True))
    centred = value_rows - average
    variance = lax.optimization_barrier(jnp.mean(centred * centred, -1, keepdims=True))
    return centred * lax.rsqrt(variance + eps_value) * gain_vec + offset

def window_regroup(value_rows, dilation):
    row_count, feature_count = value_rows.shape
    parts = value_rows.reshape(row_count // (WIN * dilation), WIN, dilation, feature_count)
    return parts.swapaxes(1, 2).reshape(row_count // WIN, WIN, feature_count)

def window_ungroup(block_list, dilation):
    group_count, window_size, feature_count = block_list.shape
    parts = block_list.reshape(group_count // dilation, dilation, window_size, feature_count)
    return parts.swapaxes(1, 2).reshape(group_count * window_size, feature_count)

@jax.checkpoint
def convolve(low_nodes, adjacent_rows, link_mask, conv_taps):
    totals = jnp.zeros(low_nodes.shape, jnp.float32)
    for tap_index in range(27):
        gathered = low_nodes[adjacent_rows[tap_index]]
        totals = totals + gathered * (link_mask[tap_index][:, None] * conv_taps[tap_index][None, :])
    return totals

def octant_block(inputs, conv_taps, gain_rows, bias_rows, qkv_mat, out_mat, up_mat, up_offset, down_mat, length_total, adjacent_rows, dilation):
    row_count, feature_count = inputs.shape
    valid_rows = (jnp.arange(row_count) < length_total).astype(jnp.float32)
    link_mask = valid_rows[None, :] * (adjacent_rows < length_total).astype(jnp.float32)
    node_count = length_total.astype(jnp.float32)
    conv_out = convolve(low(inputs), adjacent_rows, link_mask, conv_taps)
    sum_one = lax.optimization_barrier(jnp.sum(valid_rows[:, None] * conv_out, 0))
    sum_two = lax.optimization_barrier(jnp.sum(valid_rows[:, None] * conv_out * conv_out, 0))
    average = sum_one / node_count
    variance = sum_two / node_count - average * average
    hidden = inputs + (conv_out - average) * lax.rsqrt(variance + eps_value) * gain_rows[0] + bias_rows[0]
    attn_in = low(layer_norm(hidden, gain_rows[1], bias_rows[1]))
    triple = round_both(jnp.dot(attn_in, qkv_mat, precision=highest, preferred_element_type=jnp.float32))
    window_count = row_count // WIN

    def heads_of(columns):
        return window_regroup(columns, dilation).reshape(window_count, WIN, HEADS, HEAD)
    queries = heads_of(triple[:, :feature_count])
    keys_win = heads_of(triple[:, feature_count:2 * feature_count])
    values_win = heads_of(triple[:, 2 * feature_count:])
    key_bias = window_regroup(((valid_rows - 1.0) * mask_gap)[:, None], dilation)[:, None, None, :, 0]
    score_scale = 1.0 / math.sqrt(HEAD)
    scores = jnp.einsum('wihd,wjhd->whij', queries, keys_win, precision=highest) * score_scale + key_bias
    scores = low_back(scores)
    attn_probs = low(jax.nn.softmax(scores, axis=-1))
    attn_mixed = jnp.einsum('whij,wjhd->wihd', attn_probs, values_win, precision=highest)
    attn_mixed = round_both(window_ungroup(attn_mixed.reshape(window_count, WIN, feature_count), dilation))
    attn_branch = low_back(jnp.dot(attn_mixed, out_mat, precision=highest, preferred_element_type=jnp.float32) + bias_rows[3])
    hidden_two = hidden + attn_branch
    mlp_in = low(layer_norm(hidden_two, gain_rows[2], bias_rows[2]))
    pre_act = low_back(jnp.dot(mlp_in, up_mat, precision=highest, preferred_element_type=jnp.float32) + up_offset)
    activated = low(jax.nn.gelu(pre_act, approximate=False))
    mlp_branch = low_back(jnp.dot(activated, down_mat, precision=highest, preferred_element_type=jnp.float32) + bias_rows[4])
    return hidden_two + mlp_branch

def reference(node_features, cotangent, lengths, neighbours, conv_weight, norm_gains, biases, qkv_weight, out_weight, up_weight, up_bias, down_weight):
    all_params = [param.astype(jnp.float32) for param in (conv_weight, norm_gains, biases, qkv_weight, out_weight, up_weight, up_bias, down_weight)]
    first_params = [param[0] for param in all_params]
    second_params = [param[1] for param in all_params]

    def one_batch(totals, batch_items):
        inputs, grad_out, length_total, adjacent_rows = batch_items

        def first_block(value_rows, *parameter_set):
            return octant_block(value_rows, *parameter_set, length_total, adjacent_rows, 1)

        def second_block(value_rows, *parameter_set):
            return octant_block(value_rows, *parameter_set, length_total, adjacent_rows, WINDOW_DILATION)
        hidden_one, back_first = jax.vjp(first_block, inputs, *first_params)
        hidden_two, back_second = jax.vjp(second_block, hidden_one, *second_params)
        second_grads = back_second(grad_out)
        first_grads = back_first(second_grads[0])
        new_first = tuple((total + grad for total, grad in zip(totals[0], first_grads[1:])))
        new_second = tuple((total + grad for total, grad in zip(totals[1], second_grads[1:])))
        return ((new_first, new_second), (hidden_one, hidden_two, first_grads[0], second_grads[0]))
    zero_grads = tuple((jnp.zeros_like(param) for param in first_params))
    (first_totals, second_totals), (outs_one, outs_two, grads_one, grads_two) = lax.scan(one_batch, (zero_grads, zero_grads), (node_features, cotangent, lengths, neighbours))
    stacked = [jnp.stack([one_grad, two_grad]) for one_grad, two_grad in zip(first_totals, second_totals)]
    return (jnp.stack([outs_one, outs_two]), jnp.stack([grads_one, grads_two]), stacked[0], stacked[1], stacked[2], stacked[3], stacked[4], stacked[5], stacked[6], stacked[7])
```

```python
from functools import partial
import math

import jax
import jax.numpy as jnp
from jax import lax
from jax.experimental import pallas as pl
from jax.experimental.pallas import tpu as pltpu
from jax.sharding import PartitionSpec as P

HEADS = 24
HEAD = 16
WIN = 32
HALO = 64
TAPS = 27
BAND = 128
PER_BAND = BAND // HEAD
EPS = 1e-05
GAP = 10000.0
BF = jnp.bfloat16
F32 = jnp.float32
BOTH = ("section", "row")
VMEM_BYTES = 56 * 1024 * 1024

NN = (((1,), (0,)), ((), ()))
NT = (((1,), (1,)), ((), ()))
TN = (((0,), (0,)), ((), ()))


def mm(a, b, dims=NN):
    return lax.dot_general(a, b, dims, preferred_element_type=F32)


def col_sum(v):
    return jnp.sum(v, 0, keepdims=True)


def cost(us):
    return pl.CostEstimate(flops=int(us * 1.1e9), bytes_accessed=int(us * 3.6e6), transcendentals=0)


def norm_rows(v):
    mean = jnp.mean(v, -1, keepdims=True)
    centred = v - mean
    rstd = lax.rsqrt(jnp.mean(centred * centred, -1, keepdims=True) + EPS)
    return centred * rstd, rstd


def norm_rows_back(grad, gain, normed, rstd):
    dn = grad * gain
    return (dn - jnp.mean(dn, -1, keepdims=True) - normed * jnp.mean(dn * normed, -1, keepdims=True)) * rstd


def normal_cdf(u):
    k = 1.0 / (1.0 + (0.3275911 / math.sqrt(2.0)) * jnp.abs(u))
    e = jnp.exp(-0.5 * u * u)
    poly = 0.5 * 1.061405429
    for c in (-1.453152027, 1.421413741, -0.284496736, 0.254829592):
        poly = poly * k + 0.5 * c
    tail = poly * k * e
    return jnp.where(u >= 0.0, 1.0 - tail, tail), e * (1.0 / math.sqrt(2.0 * math.pi))


def place(index, dilation):
    if dilation == 1:
        return index
    return (index % WIN) * dilation + index // WIN


def near_columns(meta_ref, m, near_ref, rows, dilation, order_ref):
    sec = meta_ref[4]
    base = meta_ref[0]
    limit = meta_ref[1 + m]
    near = near_ref[0, :, pl.ds(pl.multiple_of(sec * rows, rows), rows)]
    at = base + lax.broadcasted_iota(jnp.int32, near.shape, 1)
    local = jnp.where((at < limit) & (near < limit), near - base + HALO, -1)
    local = jnp.concatenate([local, jnp.full((BAND - TAPS, rows), -1, jnp.int32)], 0).T
    if dilation == 1:
        return local
    order_ref[...] = local
    return jnp.concatenate([order_ref[pl.ds(w, WIN, stride=dilation), :] for w in range(dilation)], 0)


def fill_table(columns, tab_ref):
    span = tab_ref.shape[1]
    rows = columns.shape[0]
    lanes = lax.broadcasted_iota(jnp.int32, (rows, span), 1)
    for k in range(TAPS):
        hit = columns[:, k : k + 1] == lanes
        tab_ref[k * rows : (k + 1) * rows, :] = jnp.where(hit, 1.0, 0.0).astype(BF)


def fill_span(sec, rows, parts, ext_ref):
    if len(parts) == 2:
        full, edge = parts
        own = 2 * rows - HALO

        @pl.when(sec == 0)
        def _():
            ext_ref[:HALO] = edge[0]
            ext_ref[HALO:] = full[0, :own].astype(BF)

        @pl.when(sec != 0)
        def _():
            ext_ref[:own] = full[0, HALO:].astype(BF)
            ext_ref[own:] = edge[0]

    else:
        mid, before, after = parts
        ext_ref[:HALO] = before[0]
        ext_ref[HALO : HALO + rows] = mid[0].astype(BF)
        ext_ref[HALO + rows :] = after[0]


def pick_small(block, meta_ref, own_ref, other_ref):
    return jnp.where(meta_ref[4] == block, own_ref[0].astype(F32), other_ref[0].astype(F32))


def conv_kernel(block, dilation, parts, pins, meta_ref, *refs):
    spans, refs = refs[:parts], refs[parts:]
    near_ref, w_own, w_other, z_ref, st_ref, tab_ref, ext_ref, order_ref = refs[:3] + refs[3 + pins :]
    m = pl.program_id(0)
    rows = z_ref.shape[1]
    fill_span(meta_ref[4], rows, spans, ext_ref)
    fill_table(near_columns(meta_ref, m, near_ref, rows, dilation, order_ref), tab_ref)
    w = pick_small(block, meta_ref, w_own, w_other)
    ext = ext_ref[...]
    per = 9
    z = jnp.zeros(z_ref.shape[1:], F32)
    for c in range(TAPS // per):
        picked = mm(tab_ref[c * per * rows : (c + 1) * per * rows, :], ext)
        for t in range(per):
            k = c * per + t
            z = z + picked[t * rows : (t + 1) * rows] * w[k : k + 1, :]
    z_ref[0] = z
    index = lax.broadcasted_iota(jnp.int32, (rows, 1), 0)
    valid = meta_ref[0] + place(index, dilation) < meta_ref[1 + m]
    zv = jnp.where(valid, z, 0.0)

    @pl.when(m == 0)
    def _():
        st_ref[...] = jnp.zeros_like(st_ref)

    st_ref[0, pl.ds(m, 1), :] = col_sum(zv)
    st_ref[0, pl.ds(3 + m, 1), :] = col_sum(zv * z)


def per_batch(v):
    shape = (1,) + v.shape[1:]
    return pl.BlockSpec(shape, lambda m, *_: (m,) + (0,) * (len(shape) - 1))


def conv_forward(block, dilation, meta, spans, near, w_own, w_other, after=()):
    mb = near.shape[0]
    rows = near.shape[2] // 2
    feat = w_own.shape[2]
    return pl.pallas_call(
        partial(conv_kernel, block, dilation, len(spans), len(after)),
        grid_spec=pltpu.PrefetchScalarGridSpec(
            num_scalar_prefetch=1,
            grid=(mb,),
            in_specs=[per_batch(v) for v in (*spans, near)]
            + [whole_spec(w_own.shape)] * 2
            + [pl.BlockSpec(memory_space=pl.ANY)] * len(after),
            out_specs=[
                pl.BlockSpec((1, rows, feat), lambda m, *_: (m, 0, 0)),
                whole_spec((1, 8, feat)),
            ],
            scratch_shapes=[
                pltpu.VMEM((TAPS * rows, rows + 2 * HALO), BF),
                pltpu.VMEM((rows + 2 * HALO, feat), BF),
                pltpu.VMEM((rows, BAND), jnp.int32),
            ],
        ),
        out_shape=[
            jax.ShapeDtypeStruct((mb, rows, feat), F32),
            jax.ShapeDtypeStruct((1, 8, feat), F32),
        ],
        compiler_params=pltpu.CompilerParams(vmem_limit_bytes=VMEM_BYTES),
        cost_estimate=cost(6),
    )(meta, *spans, near, w_own, w_other, *after)


def in_node_order(v, dilation, order_ref):
    if dilation == 1:
        return v
    bands = v.shape[1] // BAND
    for c in range(bands):
        for w in range(dilation):
            order_ref[c, pl.ds(w, WIN, stride=dilation), :] = v[w * WIN : (w + 1) * WIN, c * BAND : (c + 1) * BAND]
    return jnp.concatenate([order_ref[c] for c in range(bands)], 1)


def in_window_order(v, dilation, order_ref):
    if dilation == 1:
        return v
    bands = v.shape[1] // BAND
    for c in range(bands):
        order_ref[c] = v[:, c * BAND : (c + 1) * BAND]
    return jnp.concatenate(
        [
            jnp.concatenate([order_ref[c, pl.ds(w, WIN, stride=dilation), :] for w in range(dilation)], 0)
            for c in range(bands)
        ],
        1,
    )


def conv_back_kernel(block, dilation, parts, pins, meta_ref, *refs):
    spans, refs = refs[:parts], refs[parts:]
    refs = refs[:9] + refs[9 + pins :]
    (
        near_ref, w_own, w_other, gain_own, gain_other, dh_ref, z_ref, st_ref, gst_ref,
        mid_ref, head_ref, tail_ref, taps_ref, tab_ref, ext_ref, order_ref, wtd_ref, nat_ref,
    ) = refs
    m = pl.program_id(0)
    rows, feat = z_ref.shape[1:]
    fill_span(meta_ref[4], rows, spans, ext_ref)
    fill_table(near_columns(meta_ref, m, near_ref, rows, dilation, order_ref), tab_ref)
    w_taps = pick_small(block, meta_ref, w_own, w_other)
    gain = pick_small(block, meta_ref, gain_own, gain_other)[0:1]
    inv = 1.0 / meta_ref[1 + m].astype(F32)
    pick = lambda ref, row: col_sum(ref[:, pl.ds(row, 1), :].reshape(-1, feat))
    mu = pick(st_ref, m) * inv
    var = pick(st_ref, 3 + m) * inv - mu * mu
    r = lax.rsqrt(var + EPS)
    sum_dh = pick(gst_ref, m) * gain
    sum_dhz = pick(gst_ref, 3 + m) * gain
    big_a = -0.5 * r * r * sum_dhz
    ds2 = big_a * inv
    ds1 = (-r * sum_dh - 2.0 * mu * big_a) * inv
    index = lax.broadcasted_iota(jnp.int32, (rows, 1), 0)
    valid = meta_ref[0] + place(index, dilation) < meta_ref[1 + m]
    dh = dh_ref[0]
    z = z_ref[0]
    dz = r * gain * dh + jnp.where(valid, ds1 + 2.0 * z * ds2, 0.0)
    ext = ext_ref[...]
    per = 9

    @pl.when(m == 0)
    def _():
        taps_ref[...] = jnp.zeros_like(taps_ref)

    for c in range(TAPS // per):
        picked = mm(tab_ref[c * per * rows : (c + 1) * per * rows, :], ext)
        for t in range(per):
            k = c * per + t
            taps_ref[k : k + 1, :] += col_sum(picked[t * rows : (t + 1) * rows] * dz)
            wtd_ref[k * rows : (k + 1) * rows, :] = (dz * w_taps[k : k + 1, :]).astype(BF)
    spread = mm(tab_ref[...], wtd_ref[...], TN)
    mid_ref[0] = in_node_order(dh, dilation, nat_ref) + spread[HALO : HALO + rows]
    head_ref[0] = spread[:HALO].astype(BF)
    tail_ref[0] = spread[HALO + rows :].astype(BF)


def conv_backward(block, dilation, meta, spans, near, smalls, dh, z, stats, grad_stats, after):
    mb = near.shape[0]
    rows = near.shape[2] // 2
    feat = z.shape[2]
    one = lambda *shape: pl.BlockSpec((1,) + shape, lambda m, *_: (m, 0, 0))
    return pl.pallas_call(
        partial(conv_back_kernel, block, dilation, len(spans), len(after)),
        grid_spec=pltpu.PrefetchScalarGridSpec(
            num_scalar_prefetch=1,
            grid=(mb,),
            in_specs=[per_batch(v) for v in (*spans, near)]
            + [whole_spec(v.shape) for v in smalls]
            + [per_batch(dh), per_batch(z), whole_spec(stats.shape), whole_spec(grad_stats.shape)]
            + [pl.BlockSpec(memory_space=pl.ANY)] * len(after),
            out_specs=[one(rows, feat), one(HALO, feat), one(HALO, feat), whole_spec((32, feat))],
            scratch_shapes=[
                pltpu.VMEM((TAPS * rows, rows + 2 * HALO), BF),
                pltpu.VMEM((rows + 2 * HALO, feat), BF),
                pltpu.VMEM((rows, BAND), jnp.int32),
                pltpu.VMEM((TAPS * rows, feat), BF),
                pltpu.VMEM((feat // BAND, rows, BAND), F32),
            ],
        ),
        out_shape=[
            jax.ShapeDtypeStruct((mb, rows, feat), F32),
            jax.ShapeDtypeStruct((mb, HALO, feat), BF),
            jax.ShapeDtypeStruct((mb, HALO, feat), BF),
            jax.ShapeDtypeStruct((32, feat), F32),
        ],
        compiler_params=pltpu.CompilerParams(vmem_limit_bytes=VMEM_BYTES),
        cost_estimate=cost(11),
    )(meta, *spans, near, *smalls, dh, z, stats, grad_stats, *after)


def whole_spec(shape):
    return pl.BlockSpec(shape, lambda *_: (0,) * len(shape))


def head_masks(dtype):
    lane = lax.broadcasted_iota(jnp.int32, (1, 4 * BAND), 1)
    return [jnp.where((lane % BAND) // HEAD == h, 1.0, 0.0).astype(dtype) for h in range(PER_BAND)]


def pack_heads(block, masks):
    wide = jnp.concatenate([block[w * WIN : (w + 1) * WIN] for w in range(4)], 1)
    return jnp.concatenate([wide * mask for mask in masks], 0)


def pack_rows(block):
    zero = jnp.zeros((WIN, BAND), block.dtype)
    return jnp.concatenate(
        [
            jnp.concatenate([block[w * WIN : (w + 1) * WIN] if v == w else zero for v in range(4)], 1)
            for w in range(4)
        ],
        0,
    )


def own_windows(wide):
    return jnp.concatenate([wide[w * WIN : (w + 1) * WIN, w * BAND : (w + 1) * BAND] for w in range(4)], 0)


def merge_heads(packed, masks):
    total = packed[:WIN] * masks[0]
    for h in range(1, PER_BAND):
        total = total + packed[h * WIN : (h + 1) * WIN] * masks[h]
    return jnp.concatenate([total[:, w * BAND : (w + 1) * BAND] for w in range(4)], 0)


def key_bias(meta_ref, m, dilation):
    j = lax.broadcasted_iota(jnp.int32, (WIN, BAND), 0)
    w = lax.broadcasted_iota(jnp.int32, (WIN, BAND), 1) // WIN
    pos = meta_ref[0] + (w * WIN + j if dilation == 1 else j * dilation + w)
    return jnp.where(pos < meta_ref[1 + m], 0.0, -GAP)


def fetch_weights(block, meta_ref, own, other, held, sems):
    for refs, here in ((own, True), (other, False)):

        @pl.when((meta_ref[4] == block) == here)
        def _():
            for i, ref in enumerate(refs):
                pltpu.make_async_copy(ref.at[0], held[i], sems.at[i]).start()

    return [pltpu.make_async_copy(ref.at[0], held[i], sems.at[i]) for i, ref in enumerate(own)]


def weight_scratch(weights):
    return [pltpu.VMEM(w.shape[1:], BF) for w in weights] + [pltpu.SemaphoreType.DMA((len(weights),))]


def forward_steps(dilation, meta_ref, x_of, z_ref, st_ref, gains, biases, ub, weights, loads, y_ref, kept):
    wqkv_ref, wout_ref, wup_ref, wdown_ref = weights
    h_ref, h2_ref, qkv_ref, p_ref, o_ref, g_ref, gp_ref = kept
    mb, rows, feat = z_ref.shape
    bands = feat // BAND
    hidden = wup_ref.shape[1]
    total = jnp.sum(st_ref[...], 0)
    for m in range(mb):
        inv = 1.0 / meta_ref[1 + m].astype(F32)
        mu = total[m : m + 1] * inv
        var = total[3 + m : 4 + m] * inv - mu * mu
        scale = lax.rsqrt(var + EPS) * gains[0:1]
        h = x_of(m) + (z_ref[m] - mu) * scale + biases[0:1]
        h_ref[m] = h
        normed, _ = norm_rows(h)
        a = (normed * gains[1:2] + biases[1:2]).astype(BF)
        if m == 0:
            loads[0].wait()
        qkv_ref[m] = mm(a, wqkv_ref[...]).astype(BF)
    masks = head_masks(BF)

    def group(m, carry):
        bias = key_bias(meta_ref, m, dilation)
        for b in range(bands):
            lanes = slice(b * BAND, (b + 1) * BAND)
            q = qkv_ref[m, :, b * BAND : (b + 1) * BAND] * jnp.asarray(1.0 / math.sqrt(HEAD), BF)
            k = qkv_ref[m, :, feat + b * BAND : feat + (b + 1) * BAND]
            v = qkv_ref[m, :, 2 * feat + b * BAND : 2 * feat + (b + 1) * BAND]
            s = mm(pack_heads(k, masks), pack_rows(q), NT).reshape(PER_BAND, WIN, BAND) + bias
            e = jnp.exp(s - jnp.max(s, 1, keepdims=True))
            p = (e * (1.0 / jnp.sum(e, 1, keepdims=True))).astype(BF).reshape(PER_BAND * WIN, BAND)
            p_ref[m, b] = p
            o_ref[m, :, lanes] = own_windows(mm(p, pack_heads(v, masks), TN)).astype(BF)
        return carry

    for m in range(mb):
        group(m, 0)
    flat = mb * rows
    for load in loads[1:]:
        load.wait()
    h2 = h_ref[...].reshape(flat, feat) + mm(o_ref[...].reshape(flat, feat), wout_ref[...]) + biases[3:4]
    h2_ref[...] = h2.reshape(mb, rows, feat)
    normed, _ = norm_rows(h2)
    e2 = (normed * gains[2:3] + biases[2:3]).astype(BF)
    y_ref[...] = (h2 + biases[4:5]).reshape(mb, rows, feat)
    wide = 256

    def feed(c, carry):
        at = slice(c * wide, (c + 1) * wide)
        u = mm(e2, wup_ref[:, at]) + ub[:, at]
        half, density = normal_cdf(u)
        g = (u * half).astype(BF)
        g_ref[:, at] = g
        gp_ref[:, at] = (half + u * density).astype(BF)
        y_ref[...] += mm(g, wdown_ref[at, :]).reshape(mb, rows, feat)
        return carry

    for c in range(hidden // wide):
        feed(c, 0)


def backward_steps(meta_ref, dy, z_ref, st_ref, gains, biases, weights, kept, dh_ref, gst_ref, wg_ref, small_ref, work, store):
    wqkv_ref, wout_ref, wup_ref, wdown_ref = weights
    h_ref, h2_ref, qkv_ref, p_ref, o_ref, g_ref, gp_ref = kept
    do_ref, dqkv_ref = work
    mb, rows, feat = z_ref.shape
    flat = mb * rows
    bands = feat // BAND
    hidden = wup_ref.shape[1]
    wide = feat
    blocks = hidden // wide
    dm = dy.astype(BF)
    h2 = h2_ref[...].reshape(flat, feat)
    normed2, rstd2 = norm_rows(h2)
    e2 = (normed2 * gains[2:3] + biases[2:3]).astype(BF)
    dh_ref[...] = jnp.zeros_like(dh_ref)
    small_ref[...] = jnp.zeros_like(small_ref)

    def feed(c, carry):
        at = slice(c * wide, (c + 1) * wide)
        du = (mm(dm, wdown_ref[at, :], NT) * gp_ref[:, at].astype(F32)).astype(BF)
        small_ref[8 + c : 9 + c, :] = col_sum(du.astype(F32))
        dh_ref[...] += mm(du, wup_ref[:, at], NT).reshape(mb, rows, feat)
        wg_ref[(4 + c) * feat : (5 + c) * feat, :] = mm(e2, du, TN).astype(BF)
        wg_ref[(4 + blocks + c) * feat : (5 + blocks + c) * feat, :] = mm(g_ref[:, at], dm, TN).astype(BF)
        return carry

    for c in range(blocks):
        feed(c, 0)
    store(1)
    store(2)
    de2 = dh_ref[...].reshape(flat, feat)
    small_ref[1:2, :] = col_sum(normed2 * de2)
    small_ref[4:5, :] = col_sum(de2)
    small_ref[6:7, :] = col_sum(dm.astype(F32))
    dh2 = dy + norm_rows_back(de2, gains[2:3], normed2, rstd2)
    dat = dh2.astype(BF)
    small_ref[5:6, :] = col_sum(dat.astype(F32))
    do_ref[...] = mm(dat, wout_ref[...], NT).astype(BF).reshape(mb, rows, feat)
    wg_ref[3 * feat : 4 * feat, :] = mm(o_ref[...].reshape(flat, feat), dat, TN).astype(BF)
    masks = head_masks(BF)
    masks_f = head_masks(F32)
    scale = 1.0 / math.sqrt(HEAD)

    def group(m, carry):
        for b in range(bands):
            q_at = slice(b * BAND, (b + 1) * BAND)
            k_at = slice(feat + b * BAND, feat + (b + 1) * BAND)
            v_at = slice(2 * feat + b * BAND, 2 * feat + (b + 1) * BAND)
            q = pack_rows(qkv_ref[m, :, q_at] * jnp.asarray(scale, BF))
            k = pack_heads(qkv_ref[m, :, k_at], masks)
            v = pack_heads(qkv_ref[m, :, v_at], masks)
            do = pack_rows(do_ref[m, :, q_at])
            p16 = p_ref[m, b]
            p = p16.astype(F32).reshape(PER_BAND, WIN, BAND)
            dp = mm(v, do, NT).reshape(PER_BAND, WIN, BAND)
            ds = (p * (dp - jnp.sum(p * dp, 1, keepdims=True))).astype(BF).reshape(PER_BAND * WIN, BAND)
            dqkv_ref[m, :, v_at] = merge_heads(mm(p16, do), masks_f).astype(BF)
            dqkv_ref[m, :, k_at] = merge_heads(mm(ds, q), masks_f).astype(BF)
            dqkv_ref[m, :, q_at] = (own_windows(mm(ds, k, TN)) * scale).astype(BF)
        return carry

    for m in range(mb):
        group(m, 0)
    dqkv = dqkv_ref[...].reshape(flat, 3 * feat)
    normed1, rstd1 = norm_rows(h_ref[...].reshape(flat, feat))
    a = (normed1 * gains[1:2] + biases[1:2]).astype(BF)
    for c in range(3):
        wg_ref[c * feat : (c + 1) * feat, :] = mm(a, dqkv[:, c * feat : (c + 1) * feat], TN).astype(BF)
    da = mm(dqkv, wqkv_ref[...], NT)
    small_ref[0:1, :] = col_sum(normed1 * da)
    small_ref[3:4, :] = col_sum(da)
    dh = dh2 + norm_rows_back(da, gains[1:2], normed1, rstd1)
    dh_ref[...] = dh.reshape(mb, rows, feat)
    total = jnp.sum(st_ref[...], 0)
    gst_ref[...] = jnp.zeros_like(gst_ref)
    for m in range(mb):
        inv = 1.0 / meta_ref[1 + m].astype(F32)
        mu = total[m : m + 1] * inv
        var = total[3 + m : 4 + m] * inv - mu * mu
        dh_m = dh[m * rows : (m + 1) * rows]
        gst_ref[0, m : m + 1, :] = col_sum(dh_m)
        gst_ref[0, 3 + m : 4 + m, :] = col_sum(dh_m * (z_ref[m] - mu)) * lax.rsqrt(var + EPS)


def grad_stores(meta_ref, wg_ref, keep_ref, send_ref, sems):
    feat = wg_ref.shape[1]
    half = wg_ref.shape[0] // 2
    parts = [(0, 0, 4 * feat), (0, 4 * feat, half - 4 * feat), (1, 0, half)]

    def copy(i, ref):
        which, at, count = parts[i]
        return pltpu.make_async_copy(
            wg_ref.at[pl.ds(which * half + at, count)], ref.at[pl.ds(at, count)], sems.at[i]
        )

    def start(i):
        for ref, here in ((keep_ref, True), (send_ref, False)):

            @pl.when((meta_ref[4] == parts[i][0]) == here)
            def _():
                copy(i, ref).start()

    def finish():
        start(0)
        for i in range(3):
            copy(i, keep_ref).wait()

    return start, finish


def kept_shapes(mb, rows, feat, hidden):
    return [
        ((mb, rows, feat), F32), ((mb, rows, feat), F32), ((mb, rows, 3 * feat), BF),
        ((mb, feat // BAND, PER_BAND * WIN, BAND), BF), ((mb, rows, feat), BF),
        ((mb * rows, hidden), BF), ((mb * rows, hidden), BF),
    ]


def call(us, kernel, meta, blocks, whole, outs, any_outs, scratch):
    return pl.pallas_call(
        kernel,
        grid_spec=pltpu.PrefetchScalarGridSpec(
            num_scalar_prefetch=1,
            grid=(1,),
            in_specs=[whole_spec(v.shape) for v in whole] + [pl.BlockSpec(memory_space=pl.ANY)] * len(blocks),
            out_specs=[whole_spec(shape) for shape, _ in outs] + [pl.BlockSpec(memory_space=pl.ANY)] * len(any_outs),
            scratch_shapes=scratch,
        ),
        out_shape=[jax.ShapeDtypeStruct(shape, dtype) for shape, dtype in outs + any_outs],
        compiler_params=pltpu.CompilerParams(vmem_limit_bytes=VMEM_BYTES),
        cost_estimate=cost(us),
    )(meta, *whole, *blocks)


def small_of(block, meta_ref, refs):
    gain_own, gain_other, bias_own, bias_other, ub_own, ub_other = refs
    ub = jnp.where(meta_ref[4] == block, ub_own[...].astype(F32), ub_other[...].astype(F32))
    return pick_small(block, meta_ref, gain_own, gain_other), pick_small(block, meta_ref, bias_own, bias_other), ub


def first_kernel(meta_ref, x_ref, z_ref, st_ref, *refs):
    smalls, own, other, refs = refs[:6], refs[6:10], refs[10:14], refs[14:]
    y_ref, head_ref, tail_ref, *refs = refs
    kept, held, sems, ub_ref = refs[:7], refs[7:11], refs[11], refs[12]
    loads = fetch_weights(0, meta_ref, own, other, held, sems)
    gains, biases, ub = small_of(0, meta_ref, smalls)
    ub_ref[...] = ub
    rows = z_ref.shape[1]
    own_rows = pl.ds(pl.multiple_of(meta_ref[4] * rows, rows), rows)
    forward_steps(
        1, meta_ref, lambda m: x_ref[m, own_rows, :], z_ref, st_ref, gains, biases, ub_ref, held, loads, y_ref, kept
    )
    head_ref[...] = y_ref[:, :HALO].astype(BF)
    tail_ref[...] = y_ref[:, rows - HALO :].astype(BF)


def first_forward(meta, x, z, stats, smalls, own, other):
    mb, rows, feat = z.shape
    hidden = own[2].shape[2]
    outs = [((mb, rows, feat), F32), ((mb, HALO, feat), BF), ((mb, HALO, feat), BF)] + kept_shapes(mb, rows, feat, hidden)
    return call(
        14, first_kernel, meta, (*own, *other), (x, z, stats, *smalls), outs, [],
        weight_scratch(own) + [pltpu.VMEM((1, hidden), F32)],
    )


def second_kernel(dilation, meta_ref, y0_ref, ct_ref, z_ref, st_ref, *refs):
    smalls, own, other, refs = refs[:6], refs[6:10], refs[10:14], refs[14:]
    y_ref, dh_ref, gst_ref, small_ref, keep_ref, send_ref, *refs = refs
    kept, held, sems, work, refs = refs[:7], refs[7:11], refs[11], refs[12:14], refs[14:]
    wg_ref, order_ref, out_sems, yw_ref, ub_ref = refs
    loads = fetch_weights(1, meta_ref, own, other, held, sems)
    store, finish = grad_stores(meta_ref, wg_ref, keep_ref, send_ref, out_sems)
    gains, biases, ub = small_of(1, meta_ref, smalls)
    ub_ref[...] = ub
    mb, rows, feat = z_ref.shape
    own_rows = pl.ds(pl.multiple_of(meta_ref[4] * rows, rows), rows)
    forward_steps(
        dilation, meta_ref, lambda m: in_window_order(y0_ref[m], dilation, order_ref), z_ref, st_ref, gains, biases,
        ub_ref, held, loads, yw_ref, kept,
    )
    for m in range(mb):
        y_ref[m] = in_node_order(yw_ref[m], dilation, order_ref)
    for m in range(mb):
        yw_ref[m] = in_window_order(ct_ref[m, own_rows, :], dilation, order_ref)
    dy = yw_ref[...].reshape(mb * rows, feat)
    backward_steps(
        meta_ref, dy, z_ref, st_ref, gains, biases, held, kept, dh_ref, gst_ref, wg_ref, small_ref, work, store
    )
    finish()


def grad_scratch(mb, rows, feat, hidden):
    return [
        pltpu.VMEM((mb, rows, feat), BF),
        pltpu.VMEM((mb, rows, 3 * feat), BF),
        pltpu.VMEM((4 * feat + 2 * hidden, feat), BF),
        pltpu.VMEM((feat // BAND, rows, BAND), F32),
        pltpu.SemaphoreType.DMA((3,)),
    ]


def second_both(dilation, meta, y0, ct, z, stats, smalls, own, other):
    mb, rows, feat = z.shape
    hidden = own[2].shape[2]
    half = (2 * feat + hidden, feat)
    outs = [((mb, rows, feat), F32), ((mb, rows, feat), F32), ((1, 8, feat), F32), ((16, feat), F32)]
    return call(
        25, partial(second_kernel, dilation), meta, (*own, *other), (y0, ct, z, stats, *smalls), outs,
        [(half, BF), (half, BF)],
        [pltpu.VMEM(shape, dtype) for shape, dtype in kept_shapes(mb, rows, feat, hidden)]
        + weight_scratch(own) + grad_scratch(mb, rows, feat, hidden)
        + [pltpu.VMEM((mb, rows, feat), F32), pltpu.VMEM((1, hidden), F32)],
    )


def first_back_kernel(pins, meta_ref, mid_ref, below_ref, above_ref, z_ref, st_ref, *refs):
    kept, smalls, own, other, refs = refs[:7], refs[7:13], refs[13:17], refs[17:21], refs[21 + pins :]
    dy_ref, dh_ref, gst_ref, small_ref, keep_ref, send_ref, *refs = refs
    held, sems, work, wg_ref, out_sems = refs[:4], refs[4], refs[5:7], refs[7], refs[9]
    loads = fetch_weights(0, meta_ref, own, other, held, sems)
    store, finish = grad_stores(meta_ref, wg_ref, keep_ref, send_ref, out_sems)
    gains, biases, _ = small_of(0, meta_ref, smalls)
    mb, rows, feat = z_ref.shape
    dy_ref[:, :HALO] = mid_ref[:, :HALO] + below_ref[...].astype(F32)
    dy_ref[:, HALO:] = mid_ref[:, HALO:] + above_ref[...].astype(F32)
    for load in loads:
        load.wait()
    dy = dy_ref[...].reshape(mb * rows, feat)
    backward_steps(
        meta_ref, dy, z_ref, st_ref, gains, biases, held, kept, dh_ref, gst_ref, wg_ref, small_ref, work, store
    )
    finish()


def first_backward(meta, mid, below, above, z, stats, kept, smalls, own, other, after):
    mb, rows, feat = z.shape
    hidden = own[2].shape[2]
    half = (2 * feat + hidden, feat)
    outs = [((mb, rows, feat), F32), ((mb, rows, feat), F32), ((1, 8, feat), F32), ((16, feat), F32)]
    return call(
        19, partial(first_back_kernel, len(after)), meta, (*own, *other, *after), (mid, below, above, z, stats, *kept, *smalls), outs,
        [(half, BF), (half, BF)], weight_scratch(own) + grad_scratch(mb, rows, feat, hidden),
    )


def join_kernel(meta_ref, zero_ref, one_ref, from_one_ref, from_zero_ref, out_ref, buf_ref, in_sems, out_sems):
    mb, rows = zero_ref.shape[:2]
    loads = []
    for m in range(mb):
        for at in range(2):
            loads.append((m, at, buf_ref.at[m, pl.ds(at * rows, rows)], in_sems.at[2 * m + at]))
    for sec, halves in enumerate(((zero_ref, from_one_ref), (from_zero_ref, one_ref))):

        @pl.when(meta_ref[4] == sec)
        def _():
            for m, at, target, sem in loads:
                pltpu.make_async_copy(halves[at].at[m], target, sem).start()

    stores = []
    for m, at, target, sem in loads:
        pltpu.make_async_copy(zero_ref.at[m], target, sem).wait()
        if at == 1:
            stores.append(pltpu.make_async_copy(buf_ref.at[m], out_ref.at[m], out_sems.at[m]))
            stores[-1].start()
    for copy in stores:
        copy.wait()


def exchanged(zero, one):
    return lax.ppermute(zero, "section", [(1, 0)]), lax.ppermute(one, "section", [(0, 1)])


def joined(meta, zero, one, from_one, from_zero):
    mb, rows, feat = zero.shape
    return call(
        2, join_kernel, meta, (zero, one, from_one, from_zero), (), [], [((mb, 2 * rows, feat), F32)],
        [
            pltpu.VMEM((mb, 2 * rows, feat), F32),
            pltpu.SemaphoreType.DMA((2 * mb,)), pltpu.SemaphoreType.DMA((mb,)),
        ],
    )[0]


def spread_kernel(held, into, meta_ref, *refs):
    colours, refs = refs[:2], refs[2 + into :]
    qkv_ref, out_ref, up_ref, down_ref, got_ref, wide_ref, in_sems, out_sems = refs
    feat = out_ref.shape[0]
    blocks = up_ref.shape[1] // feat
    pieces, piece = got_ref.shape[:2]
    count = colours[0].shape[1] // piece

    def load(j):
        half, rest = divmod(j, 2 * count)
        colour, at = divmod(rest, count)
        return pltpu.make_async_copy(colours[colour].at[half, pl.ds(at * piece, piece)], got_ref.at[j], in_sems.at[j])

    def target(j, side):
        half, rest = divmod(j, 2 * count)
        colour, at = divmod(rest, count)
        row = (half * 4 * count + colour * 2 * count + side * count + at) * piece
        block, at = divmod(row, feat)
        at = pl.ds(at, piece)
        if block < 3:
            return qkv_ref.at[at, pl.ds(block * feat, feat)]
        if block == 3:
            return out_ref.at[at]
        if block < 4 + blocks:
            return up_ref.at[at, pl.ds((block - 4) * feat, feat)]
        return down_ref.at[pl.ds(row - (4 + blocks) * feat, piece)]

    for j in range(pieces):
        load(j).start()
    for j in range(pieces):
        load(j).wait()
        wide_ref[j] = got_ref[j].astype(F32)
        colour = (j % (2 * count)) // count
        for bit in range(2):

            @pl.when(meta_ref[5 + colour] == bit)
            def _():
                pltpu.make_async_copy(wide_ref.at[j], target(j, bit if held else 1 - bit), out_sems.at[j]).start()

    for j in range(pieces):
        pltpu.make_async_copy(wide_ref.at[j], target(j, 0), out_sems.at[j]).wait()


def spread_grads(meta, held, colours, into, feat, hidden):
    outs = [((feat, 3 * feat), F32), ((feat, feat), F32), ((feat, hidden), F32), ((hidden, feat), F32)]
    piece = feat // 2
    pieces = 4 * colours[0].shape[1] // piece
    assert colours[0].shape[1] % piece == 0 and 2 * pieces * piece == 4 * feat + 2 * hidden
    return pl.pallas_call(
        partial(spread_kernel, held, len(into)),
        grid_spec=pltpu.PrefetchScalarGridSpec(
            num_scalar_prefetch=1,
            grid=(1,),
            in_specs=[pl.BlockSpec(memory_space=pl.ANY)] * (2 + len(into)),
            out_specs=[pl.BlockSpec(memory_space=pl.ANY)] * 4,
            scratch_shapes=[
                pltpu.VMEM((pieces, piece, feat), BF), pltpu.VMEM((pieces, piece, feat), F32),
                pltpu.SemaphoreType.DMA((pieces,)), pltpu.SemaphoreType.DMA((pieces,)),
            ],
        ),
        out_shape=[jax.ShapeDtypeStruct(shape, dtype) for shape, dtype in outs],
        input_output_aliases={3 + i: i for i in range(len(into))},
        compiler_params=pltpu.CompilerParams(vmem_limit_bytes=VMEM_BYTES),
        cost_estimate=cost(3),
    )(meta, *colours, *into)


def add_kernel(*refs):
    total = refs[0][...]
    for ref in refs[1:-1]:
        total = total + ref[...]
    refs[-1][...] = total


def added_up(parts, us):
    return pl.pallas_call(
        add_kernel,
        out_shape=jax.ShapeDtypeStruct(parts[0].shape, parts[0].dtype),
        cost_estimate=cost(us),
    )(*parts)


def on_device(
    node_features, cotangent, lengths, neighbours, conv_weight, norm_gains, biases,
    qkv_weight, out_weight, up_weight, up_bias, down_weight,
):
    sec = lax.axis_index("section")
    row = lax.axis_index("row")
    row_count = lax.axis_size("row")
    parts = 2 * row_count
    first = sec == 0
    mb, chip_rows, feat = node_features.shape
    hidden = up_bias.shape[1]
    rows = chip_rows // 2
    assert rows == BAND and mb == 3
    base = (2 * row + sec) * rows
    meta = jnp.concatenate([base[None], lengths, jnp.stack([sec] + [(row // bit) % 2 for bit in (1, 2, 4)])]).astype(jnp.int32)
    dilation = rows // WIN
    swap = [(0, 1), (1, 0)]
    bits = [1 << i for i in range(row_count.bit_length() - 1)]
    assert row_count == 1 << len(bits) and len(bits) in (4, 6)

    def swapped(v):
        return lax.ppermute(v, "section", swap)

    def device(part):
        return (part % 2) * row_count + part // 2

    forward = [(device(i), device(i + 1)) for i in range(parts - 1)]
    backward = [(j, i) for i, j in forward]
    across = [(device(2 * i + 1), device(2 * i + 2)) for i in range(row_count - 1)]
    outer = across + [(j, i) for i, j in across]

    steps = [4**i for i in range(len(bits) // 2)]

    def of_digit(v, step):
        return [v] + [lax.ppermute(v, "row", [(i, i ^ (j * step)) for i in range(row_count)]) for j in (1, 2, 3)]

    def sum_digit(v, step):
        one, two, three, four = of_digit(v, step)
        return (one + two) + (three + four)

    def sum_first(v):
        v = v + swapped(v)
        for step in steps[:-1]:
            v = sum_digit(v, step)
        return v

    def sum_all(v):
        return sum_digit(sum_first(v), steps[-1])

    def ordered(v, *ahead):
        return lax.optimization_barrier((v, ahead))[0]

    def across_bit(v, bit):
        return lax.ppermute(v, "row", [(i, i ^ bit) for i in range(row_count)])

    colour_bits = (bits, bits[1::-1] + bits[2:])

    def cut(v, bit):
        half = v.shape[-2] // 2
        at = (row // bit) % 2
        return [lax.dynamic_slice_in_dim(v, i * half, half, v.ndim - 2) for i in (at, 1 - at)]

    def added(kept, sent, bit):
        return (kept.astype(F32) + across_bit(sent, bit).astype(F32)).astype(BF)

    def halve(v, bit):
        return added(*cut(v, bit), bit)

    def double(v, bit):
        other = across_bit(v, bit)
        low = (row // bit) % 2 == 0
        return jnp.concatenate([jnp.where(low, v, other), jnp.where(low, other, v)], 1)

    def pair_sum(keep, send):
        got = swapped(send)
        half = keep.shape[0] // 2
        return [(keep[at : at + half].astype(F32) + got[at : at + half].astype(F32)).astype(BF) for at in (0, half)]

    edge = jnp.where(first, node_features[:, :HALO], node_features[:, chip_rows - HALO :]).astype(BF)
    taps = (conv_weight, swapped(conv_weight))
    own = (qkv_weight, out_weight, up_weight, down_weight)
    late, edge, _ = lax.optimization_barrier(((*own, norm_gains, biases, up_bias), edge, taps[1]))
    edge = lax.ppermute(edge, BOTH, outer)
    late = [swapped(w) for w in late]
    pairs = [(w, o) for w, o in zip((norm_gains, biases, up_bias), late[4:])]
    smalls = pairs[0] + pairs[1] + pairs[2]
    other = tuple(late[:4])

    spans0 = (node_features, edge)
    z0, st0 = conv_forward(0, 1, meta, spans0, neighbours, *taps)
    st0, other = lax.optimization_barrier((st0, other))
    st0 = sum_all(st0)
    y0, head, tail, *kept = first_forward(meta, node_features, z0, st0, smalls, own, other)
    before = lax.ppermute(tail, BOTH, forward)
    after = lax.ppermute(head, BOTH, backward)
    spans1 = (y0, before, after)
    z1, st1 = conv_forward(1, dilation, meta, spans1, neighbours, *taps)
    st1 = sum_all(st1)
    y1, dh1, gst1, small1, keep1, send1 = second_both(
        dilation, meta, y0, cotangent, z1, st1, smalls, own, other
    )
    cuts1 = [cut(part, order[0]) for part, order in zip(pair_sum(keep1, send1), colour_bits)]
    gst1 = sum_all(gst1)
    mid, head, tail, tap1 = conv_backward(
        1, dilation, meta, spans1, neighbours, taps + pairs[0], dh1, z1, st1, gst1, [sent for _, sent in cuts1]
    )
    parts1 = [added(*pair, order[0]) for pair, order in zip(cuts1, colour_bits)]
    below = lax.ppermute(tail, BOTH, forward)
    above = lax.ppermute(head, BOTH, backward)
    dx1, dh0, gst0, small0, keep0, send0 = first_backward(
        meta, mid, below, above, z0, st0, kept, smalls, own, other, parts1
    )
    cuts0 = [cut(part, order[0]) for part, order in zip(pair_sum(keep0, send0), colour_bits)]
    gst0 = [gst0, swapped(gst0)]
    gst0 = added_up(ordered(gst0, [sent for _, sent in cuts0]), 15)
    for step in steps[:-2]:
        gst0 = sum_digit(gst0, step)
    gst0 = of_digit(gst0, steps[-2])
    parts0 = [added(*pair, order[0]) for pair, order in zip(cuts0, colour_bits)]
    cuts = [cut(jnp.stack(pair), order[1]) for pair, order in zip(zip(parts0, parts1), colour_bits)]
    gst0 = added_up(ordered(gst0, [sent for _, sent in cuts]), 15)
    gst0 = sum_digit(gst0, steps[-1])
    parts = [added(ordered(kept, gst0), sent, order[1]) for (kept, sent), order in zip(cuts, colour_bits)]
    kept_z, sent_z = cut(jnp.concatenate(parts, 1), bits[2])
    mid, head, tail, tap0 = conv_backward(
        0, 1, meta, spans0, neighbours, taps + pairs[0], dh0, z0, st0, gst0, [sent_z]
    )
    small = jnp.concatenate([tap0, small0, tap1, small1], 0)
    small = small + swapped(small)
    v = added(ordered(kept_z, mid), sent_z, bits[2])
    kept_z, sent_z = cut(v, bits[3])
    head, tail, small = ordered((head, tail, small), sent_z)
    below = lax.ppermute(tail, BOTH, forward).astype(F32)
    above = lax.ppermute(head, BOTH, backward).astype(F32)
    v = added(ordered(kept_z, below, above), sent_z, bits[3])
    for bit in bits[4:]:
        v = halve(v, bit)
    theirs = swapped(jnp.where(first, v[1], v[0]))
    v = jnp.stack([jnp.where(first, v[0], theirs), jnp.where(first, theirs, v[1])])
    y0, y1, below, above, small = ordered((y0, y1, below, above, small), v)
    for step in steps[:-1]:
        small = sum_digit(small, step)
    passed_y = exchanged(y0, y1)
    dx0 = mid + jnp.concatenate([below, above], 1)
    for bit in bits[:2:-1]:
        v = double(v, bit)
    v, dx0, dx1 = lax.optimization_barrier((ordered(v, passed_y, small), dx0, dx1))
    passed_x = exchanged(dx0, dx1)
    y0, y1 = ordered((y0, y1), v)
    block_out = joined(meta, y0, y1, *passed_y)
    v = ordered(double(v, bits[2]), passed_x, block_out)
    at = v.shape[1] // 2
    held = [v[:, :at], v[:, at:]]
    dx0, dx1 = ordered((dx0, dx1), held)
    held = [double(part, order[1]) for part, order in zip(held, colour_bits)]
    input_grad = joined(meta, dx0, dx1, *passed_x)
    small = sum_digit(ordered(small, held), steps[-1])
    got = [across_bit(part, order[0]) for part, order in zip(held, colour_bits)]
    tap0, small0, tap1, small1 = small[:32], small[32:48], small[48:80], small[80:]

    mine = jnp.where(first, tap0, tap1)
    rest = jnp.where(first, small0, small1)
    bn = jnp.where(first, gst0[0], gst1[0])
    gains_out = jnp.concatenate([jnp.sum(bn[3:6], 0, keepdims=True), rest[0:2]], 0)
    biases_out = jnp.concatenate([jnp.sum(bn[0:3], 0, keepdims=True), rest[3:7]], 0)
    ub_out = rest[8 : 8 + hidden // feat].reshape(1, hidden)

    wide = spread_grads(meta, True, held, (), feat, hidden)
    qkv_out, out_out, up_out, down_out = spread_grads(meta, False, got, wide, feat, hidden)
    return (
        block_out[None], input_grad[None], mine[None, :TAPS], gains_out[None], biases_out[None],
        qkv_out[None], out_out[None], up_out[None], ub_out, down_out[None],
    )


def solution(mesh):
    placed = (
        P(None, "row", None),
        P(None, "row", None),
        P(),
        P(None, None, "row"),
        P("section", None, None),
        P("section", None, None),
        P("section", None, None),
        P("section", None, None),
        P("section", None, None),
        P("section", None, None),
        P("section", None),
        P("section", None, None),
    )
    return jax.shard_map(
        on_device,
        mesh=mesh,
        in_specs=placed,
        out_specs=(
            P("section", None, "row", None),
            P("section", None, "row", None),
            P("section", None, None),
            P("section", None, None),
            P("section", None, None),
            P("section", None, None),
            P("section", None, None),
            P("section", None, None),
            P("section", None),
            P("section", None, None),
        ),
        check_vma=False,
    )
```
